32 devices in a mesh: row: 8 (over y, x, core), col: 4 (over z).
Axes of the slice: x: 2, y: 2, z: 4, core: 2. Of those that a mesh axis runs over, the one named last changes fastest.
Arguments:
- w_cycle: float32 [2048, 16384], P('col', 'row'), may hold values from -0.125 to 0.125
- amps: float32 [32, 512, 2048], P('col', 'row'), may hold values from -18 to 18
- eps_occ: float32 [32], replicated, may hold values from -3 to -0.3
- eps_vir: float32 [512], replicated, may hold values from 0.3 to 3
- occ_map: int32 [4], replicated, may hold values from 0 to 31
- vir_perm: int32 [512], replicated, may hold values from 0 to 511, each once
Outputs:
- cycle: float32 [16384, 16384], P('row', 'col')
The draws below stay inside these ranges and needn't reach their ends.
Inputs may be any that keep to these rules, and one draw needn't show every extreme that they name: `occ_map`: each window index names one occupied orbital. `vir_perm`: each virtual orbital appears once.
All inputs are finite; a program needn't handle non-finite values.
Results may differ from the reference program's by a relative error of at most 0.000071.
Values sent between devices are 32-bit elements; how exact they have to be, the bound alone decides.
A program may use at most 192 MiB of HBM per device.

```python
import jax
import jax.numpy as jnp
from jax import lax

OCC = 32
VIR = 512
KW = 4
CK = 2048
ORDER = 16384


def set_ends(array, own_key, smallest, high):
    spot = [jax.random.randint(jax.random.fold_in(own_key, axis), (), 0, length) for axis, length in enumerate(array.shape)]
    widest = array.shape.index(max(array.shape))
    neighbour = spot[:widest] + [(spot[widest] + 1) % array.shape[widest]] + spot[widest + 1:]
    return array.at[tuple(spot)].set(smallest).at[tuple(neighbour)].set(high)


def block_scale(stream_key, shape, pieces, least, largest):
    loudness = 1.0
    for axis_at, blocks in pieces:
        steps = jax.random.uniform(jax.random.fold_in(jax.random.fold_in(stream_key, 6), axis_at), (blocks,), jnp.float32, least / len(pieces), largest / len(pieces))
        loudness = loudness * jnp.repeat(jnp.exp(steps), shape[axis_at] // blocks).reshape((-1,) + (1,) * (len(shape) - 1 - axis_at))
    return loudness


def bell_draw(stream_key, shape, spread, reach, pieces=(), kind=jnp.bfloat16):
    drawn = spread * jax.random.normal(stream_key, shape, jnp.float32)
    if pieces:
        drawn = drawn * block_scale(stream_key, shape, pieces, -0.22, 0.18)
    return jnp.clip(drawn, -reach, reach).astype(kind)


def setup_inputs(seed: int = 0) -> dict:
    keys = jax.random.split(jax.random.key(seed), 7)
    return {
        "w_cycle": bell_draw(keys[0], (CK, ORDER), CK ** -0.5, 0.125, ((0, 4), (1, 8)), jnp.float32),
        "amps": bell_draw(keys[1], (OCC, VIR, CK), 3.0, 18.0, ((0, 4), (1, 8)), jnp.float32),
        "eps_occ": jnp.clip(jax.random.uniform(keys[2], (OCC,), jnp.float32, -3.0, -0.3), -3.0, -0.3),
        "eps_vir": jnp.clip(jax.random.uniform(keys[3], (VIR,), jnp.float32, 0.3, 3.0), 0.3, 3.0),
        "occ_map": set_ends(jax.random.randint(keys[4], (KW,), 0, OCC), jax.random.fold_in(keys[4], 1), 0, OCC - 1).astype(jnp.int32),
        "vir_perm": jax.random.permutation(keys[5], VIR).astype(jnp.int32),
    }


def reference(w_cycle, amps, eps_occ, eps_vir, occ_map, vir_perm):
    vir_energy = eps_vir[vir_perm]
    occ_energy = eps_occ[occ_map]
    pair_energy = (vir_energy[None, :] - occ_energy[:, None]).reshape(-1)
    denominator = pair_energy[None, None, :] + vir_energy[None, :, None] - eps_occ[:, None, None]
    scaled = amps / denominator
    columns = scaled.reshape(OCC * VIR, KW * VIR)
    return lax.dot_general(w_cycle, columns, (((0,), (1,)), ((), ())),
                           precision=lax.Precision.HIGHEST,
                           preferred_element_type=jnp.float32)
```

```python
import functools

import jax
import jax.numpy as jnp
from jax import lax
from jax.experimental import pallas as pl
from jax.experimental.pallas import tpu as pltpu
from jax.sharding import PartitionSpec as P

MESH = pl.DeviceIdType.MESH
LIMIT = 56 * 1024 * 1024


def gather_kernel(amps, whole, own_sem, send, recv):
    me = lax.axis_index("row")
    col = lax.axis_index("col")
    core = lax.rem(me, 2)
    x = lax.rem(me // 2, 2)
    y = me // 4
    sibling = me + 1 - 2 * core
    beside = me + 2 - 4 * x
    across = me + 4 - 8 * y
    corner = beside + across - me
    for peer in (sibling, beside, across):
        pl.semaphore_signal(
            pltpu.get_barrier_semaphore(), inc=1, device_id=(peer, col), device_id_type=MESH
        )
    pl.semaphore_wait(pltpu.get_barrier_semaphore(), 3)

    rows = amps.shape[1]
    js = amps.shape[0]
    half = js // 2

    def slot(owner, first, count):
        return whole.at[pl.ds(first, count), pl.ds(pl.multiple_of(owner * rows, 8), rows), :]

    def remote(k, src, dst, peer):
        copy = pltpu.make_async_remote_copy(
            src_ref=src,
            dst_ref=dst,
            send_sem=send.at[k],
            recv_sem=recv.at[k],
            device_id=(peer, col),
            device_id_type=MESH,
        )
        copy.start()
        return copy

    def forward(k, owner, first, count, peer):
        return remote(k, slot(owner, first, count), slot(owner, first, count), peer)

    to_x = remote(0, amps, slot(me, 0, js), beside)
    to_y = remote(1, amps, slot(me, 0, js), across)
    to_s = remote(2, amps, slot(me, 0, js), sibling)
    own = pltpu.make_async_copy(amps, slot(me, 0, js), own_sem)
    own.start()
    to_x.wait_recv()
    low = forward(3, beside, 0, half, across)
    s_x = forward(4, beside, 0, js, sibling)
    to_y.wait_recv()
    high = forward(5, across, half, js - half, beside)
    s_y = forward(6, across, 0, js, sibling)
    low.wait_recv()
    s_low = forward(7, corner, 0, half, sibling)
    high.wait_recv()
    s_high = forward(8, corner, half, js - half, sibling)
    for copy in (to_s, s_x, s_y, s_low, s_high):
        copy.wait_recv()
    for copy in (to_x, to_y, to_s, low, s_x, high, s_y, s_low, s_high):
        copy.wait_send()
    own.wait()


def gather_amps(amps, row_count):
    js, bs, cks = amps.shape
    return pl.pallas_call(
        gather_kernel,
        out_shape=jax.ShapeDtypeStruct((js, bs * row_count, cks), jnp.float32),
        in_specs=[pl.BlockSpec(memory_space=pl.ANY)],
        out_specs=pl.BlockSpec(memory_space=pl.ANY),
        scratch_shapes=[
            pltpu.SemaphoreType.DMA(()),
            pltpu.SemaphoreType.DMA((9,)),
            pltpu.SemaphoreType.DMA((9,)),
        ],
        compiler_params=pltpu.CompilerParams(
            collective_id=0, has_side_effects=True, vmem_limit_bytes=LIMIT
        ),
        name="gather_amps",
    )(amps)


def scale_kernel(j_energy, amps, pair, b_energy, high, low):
    base = pair[...] + b_energy[...]
    scaled = amps[0] / (base - j_energy[pl.program_id(0)])
    top = scaled.astype(jnp.bfloat16)
    high[0] = top
    low[0] = (scaled - top.astype(jnp.float32)).astype(jnp.bfloat16)


def scale_split(amps, pair, b_energy, j_energy):
    js, bs, cks = amps.shape
    nb = min(bs, 256)
    block = pl.BlockSpec((1, nb, cks), lambda j, b: (j, b, 0))
    shape = jax.ShapeDtypeStruct(amps.shape, jnp.bfloat16)
    return pl.pallas_call(
        scale_kernel,
        grid=(js, bs // nb),
        out_shape=(shape, shape),
        in_specs=[
            pl.BlockSpec(memory_space=pltpu.SMEM),
            block,
            pl.BlockSpec((1, cks), lambda j, b: (0, 0)),
            pl.BlockSpec((nb, 1), lambda j, b: (b, 0)),
        ],
        out_specs=(block, block),
        compiler_params=pltpu.CompilerParams(vmem_limit_bytes=LIMIT),
        cost_estimate=pl.CostEstimate(
            flops=8 * amps.size, bytes_accessed=8 * amps.size, transcendentals=0
        ),
        name="scale_split",
    )(j_energy, amps, pair.reshape(1, cks), b_energy.reshape(bs, 1))


def product_kernel(w, high, low, *rest):
    out, w_high, w_low = rest[-3:]
    cks = w.shape[0]

    @pl.when(pl.program_id(0) == 0)
    def _():
        step = min(cks, 256)

        def turn(i, carry):
            rows = pl.ds(pl.multiple_of(i * step, step), step)
            part = w[rows, :].T
            top = part.astype(jnp.bfloat16)
            w_high[:, rows] = top
            w_low[:, rows] = (part - top.astype(jnp.float32)).astype(jnp.bfloat16)
            return carry

        lax.fori_loop(0, cks // step, turn, 0)

    def dot(a, b):
        return lax.dot_general(
            a, b, (((1,), (1,)), ((), ())), preferred_element_type=jnp.float32
        )

    top = high[...]
    out[...] = (
        dot(w_low[...], top) + dot(w_high[...], low[...])
    ) + dot(w_high[...], top)


def product(w, high, low, out, first, rows_out):
    cks, count = w.shape
    columns = high.shape[0]
    nb = min(columns, 512)
    t_block = pl.BlockSpec((nb, cks), lambda n: (n, 0))
    specs = [pl.BlockSpec((cks, count), lambda n: (0, 0)), t_block, t_block]
    args = [w, high, low]
    aliases = {}
    if out is not None:
        specs.append(pl.BlockSpec(memory_space=pl.ANY))
        args.append(out)
        aliases = {3: 0}
    return pl.pallas_call(
        product_kernel,
        grid=(columns // nb,),
        out_shape=jax.ShapeDtypeStruct((rows_out, columns), jnp.float32),
        in_specs=specs,
        out_specs=pl.BlockSpec((count, nb), lambda n: (first // count, n)),
        scratch_shapes=[
            pltpu.VMEM((count, cks), jnp.bfloat16),
            pltpu.VMEM((count, cks), jnp.bfloat16),
        ],
        input_output_aliases=aliases,
        compiler_params=pltpu.CompilerParams(vmem_limit_bytes=LIMIT),
        cost_estimate=pl.CostEstimate(
            flops=6 * cks * count * columns,
            bytes_accessed=4 * (cks * count + cks * columns + count * columns),
            transcendentals=0,
        ),
        name="product",
    )(*args)


def lookup(indices, table):
    chosen = indices[:, None] == jnp.arange(table.shape[0], dtype=jnp.int32)[None, :]
    return jnp.sum(jnp.where(chosen, table[None, :], 0.0), axis=1)


def body(row_count, w_cycle, amps, eps_occ, eps_vir, occ_map, vir_perm):
    js = amps.shape[0]
    rows_out = w_cycle.shape[1]
    unit = rows_out // 8
    sizes = [2 * unit, 2 * unit, 2 * unit, unit, unit]
    starts = [sum(sizes[:k]) for k in range(len(sizes))]
    gathered = [
        lax.all_gather(w_cycle[:, s : s + n], "col", axis=0, tiled=True)
        for s, n in zip(starts, sizes)
    ]
    vir_energy = lookup(vir_perm, eps_vir)
    occ_energy = lookup(occ_map, eps_occ)
    pair = (vir_energy[None, :] - occ_energy[:, None]).reshape(-1)
    j_energy = lax.dynamic_slice_in_dim(eps_occ, lax.axis_index("col") * js, js)
    if row_count == 8 and js % 2 == 0:
        whole = gather_amps(amps, row_count)
    else:
        whole = lax.all_gather(amps, "row", axis=1, tiled=True)
    high, low = scale_split(whole, pair, vir_energy, j_energy)
    columns = whole.shape[0] * whole.shape[1]
    high = high.reshape(columns, high.shape[2])
    low = low.reshape(columns, low.shape[2])
    out = None
    for s, w in zip(starts, gathered):
        out = product(w, high, low, out, s, rows_out)
    return out


def solution(mesh):
    placed = (P("col", "row"), P("col", "row", None), P(), P(), P(), P())
    return jax.shard_map(
        functools.partial(body, mesh.shape["row"]),
        mesh=mesh,
        in_specs=placed,
        out_specs=P("row", "col"),
        check_vma=False,
    )
```

```python
import functools

import jax
import jax.numpy as jnp
from jax import lax
from jax.experimental import pallas as pl
from jax.experimental.pallas import tpu as pltpu
from jax.sharding import PartitionSpec as P

MESH = pl.DeviceIdType.MESH
LIMIT = 56 * 1024 * 1024


def gather_kernel(cols, amps, w, whole, w_whole, own_sem, send, recv, w_own_sem, w_send, w_recv):
    me = lax.axis_index("row")
    col = lax.axis_index("col")
    core = lax.rem(me, 2)
    x = lax.rem(me // 2, 2)
    y = me // 4
    sibling = me + 1 - 2 * core
    beside = me + 2 - 4 * x
    across = me + 4 - 8 * y
    corner = beside + across - me
    for peer in (sibling, beside, across):
        pl.semaphore_signal(
            pltpu.get_barrier_semaphore(), inc=1, device_id=(peer, col), device_id_type=MESH
        )
    for d in range(1, cols):
        pl.semaphore_signal(
            pltpu.get_barrier_semaphore(),
            inc=1,
            device_id=(me, lax.rem(col + d, cols)),
            device_id_type=MESH,
        )
    pl.semaphore_wait(pltpu.get_barrier_semaphore(), 3 + cols - 1)

    rows = amps.shape[1]
    js = amps.shape[0]
    half = js // 2

    def slot(owner, first, count):
        return whole.at[pl.ds(first, count), pl.ds(pl.multiple_of(owner * rows, 8), rows), :]

    def remote(k, src, dst, peer):
        copy = pltpu.make_async_remote_copy(
            src_ref=src,
            dst_ref=dst,
            send_sem=send.at[k],
            recv_sem=recv.at[k],
            device_id=(peer, col),
            device_id_type=MESH,
        )
        copy.start()
        return copy

    def forward(k, owner, first, count, peer):
        return remote(k, slot(owner, first, count), slot(owner, first, count), peer)

    to_x = remote(0, amps, slot(me, 0, js), beside)
    to_y = remote(1, amps, slot(me, 0, js), across)
    to_s = remote(2, amps, slot(me, 0, js), sibling)
    own = pltpu.make_async_copy(amps, slot(me, 0, js), own_sem)
    own.start()
    depth = w.shape[0]
    w_from = w.at[:, pl.ds(0, w_whole.shape[1])]
    w_slot = w_whole.at[pl.ds(pl.multiple_of(col * depth, 8), depth), :]
    w_copies = []
    for d in range(1, cols):
        copy = pltpu.make_async_remote_copy(
            src_ref=w_from,
            dst_ref=w_slot,
            send_sem=w_send.at[d - 1],
            recv_sem=w_recv.at[d - 1],
            device_id=(me, lax.rem(col + d, cols)),
            device_id_type=MESH,
        )
        copy.start()
        w_copies.append(copy)
    w_own = pltpu.make_async_copy(w_from, w_slot, w_own_sem)
    w_own.start()
    to_x.wait_recv()
    low = forward(3, beside, 0, half, across)
    s_x = forward(4, beside, 0, js, sibling)
    to_y.wait_recv()
    high = forward(5, across, half, js - half, beside)
    s_y = forward(6, across, 0, js, sibling)
    low.wait_recv()
    s_low = forward(7, corner, 0, half, sibling)
    high.wait_recv()
    s_high = forward(8, corner, half, js - half, sibling)
    for copy in (to_s, s_x, s_y, s_low, s_high):
        copy.wait_recv()
    for copy in (to_x, to_y, to_s, low, s_x, high, s_y, s_low, s_high):
        copy.wait_send()
    own.wait()
    for copy in w_copies:
        copy.wait_recv()
    for copy in w_copies:
        copy.wait_send()
    w_own.wait()


def gather_amps(amps, w, count, row_count, cols):
    js, bs, cks = amps.shape
    return pl.pallas_call(
        functools.partial(gather_kernel, cols),
        out_shape=(
            jax.ShapeDtypeStruct((js, bs * row_count, cks), jnp.float32),
            jax.ShapeDtypeStruct((w.shape[0] * cols, count), jnp.float32),
        ),
        in_specs=[pl.BlockSpec(memory_space=pl.ANY)] * 2,
        out_specs=(pl.BlockSpec(memory_space=pl.ANY),) * 2,
        scratch_shapes=[
            pltpu.SemaphoreType.DMA(()),
            pltpu.SemaphoreType.DMA((9,)),
            pltpu.SemaphoreType.DMA((9,)),
            pltpu.SemaphoreType.DMA(()),
            pltpu.SemaphoreType.DMA((cols - 1,)),
            pltpu.SemaphoreType.DMA((cols - 1,)),
        ],
        compiler_params=pltpu.CompilerParams(
            collective_id=0, has_side_effects=True, vmem_limit_bytes=LIMIT
        ),
        name="gather_amps",
    )(amps, w)


def scale_kernel(j_energy, amps, pair, b_energy, high, low):
    base = pair[...] + b_energy[...]
    denominator = base - j_energy[pl.program_id(0)]
    inverse = pl.reciprocal(denominator, approx=True)
    inverse = inverse * (2.0 - denominator * inverse)
    inverse = inverse + inverse * (1.0 - denominator * inverse)
    scaled = amps[0] * inverse
    top = scaled.astype(jnp.bfloat16)
    high[0] = top
    low[0] = (scaled - top.astype(jnp.float32)).astype(jnp.bfloat16)


def scale_split(amps, pair, b_energy, j_energy):
    js, bs, cks = amps.shape
    nb = min(bs, 256)
    block = pl.BlockSpec((1, nb, cks), lambda j, b: (j, b, 0))
    shape = jax.ShapeDtypeStruct(amps.shape, jnp.bfloat16)
    return pl.pallas_call(
        scale_kernel,
        grid=(js, bs // nb),
        out_shape=(shape, shape),
        in_specs=[
            pl.BlockSpec(memory_space=pltpu.SMEM),
            block,
            pl.BlockSpec((1, cks), lambda j, b: (0, 0)),
            pl.BlockSpec((nb, 1), lambda j, b: (b, 0)),
        ],
        out_specs=(block, block),
        compiler_params=pltpu.CompilerParams(vmem_limit_bytes=LIMIT),
        cost_estimate=pl.CostEstimate(
            flops=8 * amps.size, bytes_accessed=8 * amps.size, transcendentals=0
        ),
        name="scale_split",
    )(j_energy, amps, pair.reshape(1, cks), b_energy.reshape(bs, 1))


def product_kernel(parts, *refs):
    ws = refs[:parts]
    high, low = refs[parts : parts + 2]
    out, w_high, w_low = refs[-3:]
    cks, count = ws[0].shape

    @pl.when(pl.program_id(0) == 0)
    def _():
        step = min(cks, 256)

        def turn(i, carry):
            rows = pl.ds(pl.multiple_of(i * step, step), step)
            for k, w in enumerate(ws):
                part = w[rows, :].T
                top = part.astype(jnp.bfloat16)
                at = pl.ds(k * count, count)
                w_high[at, rows] = top
                w_low[at, rows] = (part - top.astype(jnp.float32)).astype(jnp.bfloat16)
            return carry

        lax.fori_loop(0, cks // step, turn, 0)

    def dot(a, b):
        return lax.dot_general(
            a, b, (((1,), (1,)), ((), ())), preferred_element_type=jnp.float32
        )

    top = high[...]
    out[...] = (
        dot(w_low[...], top) + dot(w_high[...], low[...])
    ) + dot(w_high[...], top)


def product(ws, high, low, out, first, rows_out):
    cks, each = ws[0].shape
    count = each * len(ws)
    columns = high.shape[0]
    nb = min(columns, 512)
    t_block = pl.BlockSpec((nb, cks), lambda n: (n, 0))
    w_block = pl.BlockSpec((cks, each), lambda n: (0, 0), pipeline_mode=pl.Buffered(1))
    specs = [w_block] * len(ws) + [t_block, t_block]
    args = [*ws, high, low]
    aliases = {}
    if out is not None:
        specs.append(pl.BlockSpec(memory_space=pl.ANY))
        args.append(out)
        aliases = {len(ws) + 2: 0}
    return pl.pallas_call(
        functools.partial(product_kernel, len(ws)),
        grid=(columns // nb,),
        out_shape=jax.ShapeDtypeStruct((rows_out, columns), jnp.float32),
        in_specs=specs,
        out_specs=pl.BlockSpec((count, nb), lambda n: (first // count, n)),
        scratch_shapes=[
            pltpu.VMEM((count, cks), jnp.bfloat16),
            pltpu.VMEM((count, cks), jnp.bfloat16),
        ],
        input_output_aliases=aliases,
        compiler_params=pltpu.CompilerParams(vmem_limit_bytes=LIMIT),
        cost_estimate=pl.CostEstimate(
            flops=6 * cks * count * columns,
            bytes_accessed=4 * (cks * count + cks * columns + count * columns),
            transcendentals=0,
        ),
        name="product",
    )(*args)


def lookup(indices, table):
    chosen = indices[:, None] == jnp.arange(table.shape[0], dtype=jnp.int32)[None, :]
    return jnp.sum(jnp.where(chosen, table[None, :], 0.0), axis=1)


def body(row_count, col_count, w_cycle, amps, eps_occ, eps_vir, occ_map, vir_perm):
    js = amps.shape[0]
    rows_out = w_cycle.shape[1]
    unit = rows_out // 8
    direct = row_count == 8 and js % 2 == 0
    sizes = [2 * unit, 2 * unit, 2 * unit, unit, unit]
    starts = [sum(sizes[:k]) for k in range(len(sizes))]
    gathered = [
        None
        if direct and s == 0
        else lax.all_gather(w_cycle[:, s : s + n], "col", axis=0, tiled=True)
        for s, n in zip(starts, sizes)
    ]
    vir_energy = lookup(vir_perm, eps_vir)
    occ_energy = lookup(occ_map, eps_occ)
    pair = (vir_energy[None, :] - occ_energy[:, None]).reshape(-1)
    j_energy = lax.dynamic_slice_in_dim(eps_occ, lax.axis_index("col") * js, js)
    if direct:
        whole, gathered[0] = gather_amps(amps, w_cycle, sizes[0], row_count, col_count)
    else:
        whole = lax.all_gather(amps, "row", axis=1, tiled=True)
    high, low = scale_split(whole, pair, vir_energy, j_energy)
    columns = whole.shape[0] * whole.shape[1]
    high = high.reshape(columns, high.shape[2])
    low = low.reshape(columns, low.shape[2])
    out = product(gathered[:2], high, low, None, 0, rows_out)
    for s, w in zip(starts[2:], gathered[2:]):
        out = product([w], high, low, out, s, rows_out)
    return out


def solution(mesh):
    placed = (P("col", "row"), P("col", "row", None), P(), P(), P(), P())
    return jax.shard_map(
        functools.partial(body, mesh.shape["row"], mesh.shape["col"]),
        mesh=mesh,
        in_specs=placed,
        out_specs=P("row", "col"),
        check_vma=False,
    )
```

```python
import functools

import jax
import jax.numpy as jnp
from jax import lax
from jax.experimental import pallas as pl
from jax.experimental.pallas import tpu as pltpu
from jax.sharding import PartitionSpec as P

MESH = pl.DeviceIdType.MESH
LIMIT = 56 * 1024 * 1024


def gather_kernel(amps, whole, own_sem, send, recv):
    me = lax.axis_index("row")
    col = lax.axis_index("col")
    core = lax.rem(me, 2)
    x = lax.rem(me // 2, 2)
    y = me // 4
    sibling = me + 1 - 2 * core
    beside = me + 2 - 4 * x
    across = me + 4 - 8 * y
    corner = beside + across - me
    for peer in (sibling, beside, across):
        pl.semaphore_signal(
            pltpu.get_barrier_semaphore(), inc=1, device_id=(peer, col), device_id_type=MESH
        )
    pl.semaphore_wait(pltpu.get_barrier_semaphore(), 3)

    rows = amps.shape[1]
    js = amps.shape[0]
    half = js // 2

    def slot(owner, first, count):
        return whole.at[pl.ds(first, count), pl.ds(pl.multiple_of(owner * rows, 8), rows), :]

    def remote(k, src, dst, peer):
        copy = pltpu.make_async_remote_copy(
            src_ref=src,
            dst_ref=dst,
            send_sem=send.at[k],
            recv_sem=recv.at[k],
            device_id=(peer, col),
            device_id_type=MESH,
        )
        copy.start()
        return copy

    def forward(k, owner, first, count, peer):
        return remote(k, slot(owner, first, count), slot(owner, first, count), peer)

    to_x = remote(0, amps, slot(me, 0, js), beside)
    to_y = remote(1, amps, slot(me, 0, js), across)
    to_s = remote(2, amps, slot(me, 0, js), sibling)
    own = pltpu.make_async_copy(amps, slot(me, 0, js), own_sem)
    own.start()
    to_x.wait_recv()
    low = forward(3, beside, 0, half, across)
    s_x = forward(4, beside, 0, js, sibling)
    to_y.wait_recv()
    high = forward(5, across, half, js - half, beside)
    s_y = forward(6, across, 0, js, sibling)
    low.wait_recv()
    s_low = forward(7, corner, 0, half, sibling)
    high.wait_recv()
    s_high = forward(8, corner, half, js - half, sibling)
    for copy in (to_s, s_x, s_y, s_low, s_high):
        copy.wait_recv()
    for copy in (to_x, to_y, to_s, low, s_x, high, s_y, s_low, s_high):
        copy.wait_send()
    own.wait()


def gather_amps(amps, row_count):
    js, bs, cks = amps.shape
    return pl.pallas_call(
        gather_kernel,
        out_shape=jax.ShapeDtypeStruct((js, bs * row_count, cks), jnp.float32),
        in_specs=[pl.BlockSpec(memory_space=pl.ANY)],
        out_specs=pl.BlockSpec(memory_space=pl.ANY),
        scratch_shapes=[
            pltpu.SemaphoreType.DMA(()),
            pltpu.SemaphoreType.DMA((9,)),
            pltpu.SemaphoreType.DMA((9,)),
        ],
        compiler_params=pltpu.CompilerParams(
            collective_id=0, has_side_effects=True, vmem_limit_bytes=LIMIT
        ),
        name="gather_amps",
    )(amps)


def product_kernel(first, w, *refs):
    if first:
        t, out, high, low, w_high, w_low = refs
        top = t[...].astype(jnp.bfloat16)
        high[...] = top
        low[...] = (t[...] - top.astype(jnp.float32)).astype(jnp.bfloat16)
    else:
        high, low, _, out, w_high, w_low = refs
    cks = w.shape[0]

    @pl.when(pl.program_id(0) == 0)
    def _():
        step = min(cks, 256)

        def turn(i, carry):
            rows = pl.ds(pl.multiple_of(i * step, step), step)
            part = w[rows, :].T
            top = part.astype(jnp.bfloat16)
            w_high[:, rows] = top
            w_low[:, rows] = (part - top.astype(jnp.float32)).astype(jnp.bfloat16)
            return carry

        lax.fori_loop(0, cks // step, turn, 0)

    def dot(a, b):
        return lax.dot_general(
            a, b, (((1,), (1,)), ((), ())), preferred_element_type=jnp.float32
        )

    top = high[...]
    out[...] = (
        dot(w_low[...], top) + dot(w_high[...], low[...])
    ) + dot(w_high[...], top)


def product(w, t, out, start, rows_out):
    cks, count = w.shape
    columns = t[0].shape[0]
    nb = min(columns, 512)
    first = out is None
    t_block = pl.BlockSpec((nb, cks), lambda n: (n, 0))
    w_block = pl.BlockSpec((cks, count), lambda n: (0, 0), pipeline_mode=pl.Buffered(1))
    shapes = [jax.ShapeDtypeStruct((rows_out, columns), jnp.float32)]
    outs = [pl.BlockSpec((count, nb), lambda n: (start // count, n))]
    specs = [w_block] + [t_block] * len(t)
    args = [w, *t]
    aliases = {}
    if first:
        shapes += [jax.ShapeDtypeStruct((columns, cks), jnp.bfloat16)] * 2
        outs += [t_block] * 2
    else:
        specs.append(pl.BlockSpec(memory_space=pl.ANY))
        args.append(out)
        aliases = {3: 0}
    return pl.pallas_call(
        functools.partial(product_kernel, first),
        grid=(columns // nb,),
        out_shape=shapes,
        in_specs=specs,
        out_specs=outs,
        scratch_shapes=[
            pltpu.VMEM((count, cks), jnp.bfloat16),
            pltpu.VMEM((count, cks), jnp.bfloat16),
        ],
        input_output_aliases=aliases,
        compiler_params=pltpu.CompilerParams(vmem_limit_bytes=LIMIT),
        cost_estimate=pl.CostEstimate(
            flops=6 * cks * count * columns,
            bytes_accessed=4 * (cks * count + cks * columns + count * columns),
            transcendentals=0,
        ),
        name="product",
    )(*args)


def lookup(indices, table):
    chosen = indices[:, None] == jnp.arange(table.shape[0], dtype=jnp.int32)[None, :]
    return jnp.sum(jnp.where(chosen, table[None, :], 0.0), axis=1)


def body(row_count, w_cycle, amps, eps_occ, eps_vir, occ_map, vir_perm):
    js = amps.shape[0]
    rows_out = w_cycle.shape[1]
    unit = rows_out // 8
    sizes = [4 * unit, 3 * unit, unit]
    starts = [4 * unit, 0, 3 * unit]
    gathered = [
        lax.all_gather(w_cycle[:, s : s + n], "col", axis=0, tiled=True)
        for s, n in zip(starts, sizes)
    ]
    vir_energy = lookup(vir_perm, eps_vir)
    occ_energy = lookup(occ_map, eps_occ)
    pair = (vir_energy[None, :] - occ_energy[:, None]).reshape(-1)
    j_energy = lax.dynamic_slice_in_dim(eps_occ, lax.axis_index("col") * js, js)
    bs = amps.shape[1]
    b_energy = lax.dynamic_slice_in_dim(vir_energy, lax.axis_index("row") * bs, bs)
    denominator = pair[None, None, :] + b_energy[None, :, None] - j_energy[:, None, None]
    scaled = amps / denominator
    if row_count == 8 and js % 2 == 0:
        whole = gather_amps(scaled, row_count)
    else:
        whole = lax.all_gather(scaled, "row", axis=1, tiled=True)
    columns = whole.shape[0] * whole.shape[1]
    whole = whole.reshape(columns, whole.shape[2])
    out, high, low = product(gathered[0], [whole], None, starts[0], rows_out)
    for s, w in zip(starts[1:], gathered[1:]):
        (out,) = product(w, [high, low], out, s, rows_out)
    return out


def solution(mesh):
    placed = (P("col", "row"), P("col", "row", None), P(), P(), P(), P())
    return jax.shard_map(
        functools.partial(body, mesh.shape["row"]),
        mesh=mesh,
        in_specs=placed,
        out_specs=P("row", "col"),
        check_vma=False,
    )
```
